256 devices in a mesh: dp: 16 (over y_lo, x, core), seq: 8 (over z), enc: 2 (over y_hi).
Axes of the slice: x: 4, y: 4 (y_hi: 2, y_lo: 2; y = y_hi * 2 + y_lo), z: 8, core: 2. Of those that a mesh axis runs over, the one named last changes fastest.
Arguments:
- image_qkv: bfloat16 [32, 1024, 4608], P(('dp', 'enc'), 'seq'), may hold values from -7 to 7
- residual: bfloat16 [32, 1024, 2432], P(('dp', 'enc'), 'seq'), may hold values from -1.5 to 1.5
- gate: float32 [32, 2432], P(('dp', 'enc')), may hold values from 0.5 to 2
- cotangent: bfloat16 [32, 1024, 2432], P(('dp', 'enc'), 'seq'), may hold values from -6 to 6
- t5_states: bfloat16 [32, 256, 4096], P('dp', 'seq', 'enc'), may hold values from -6 to 6
- text_weight: bfloat16 [2, 4096, 1536], P(None, 'enc', 'seq'), may hold values from -0.09375 to 0.09375
- out_weight: bfloat16 [1536, 2432], P(('dp', 'seq', 'enc')), may hold values from -0.15625 to 0.15625
- caption_len: int32 [32], P(('dp', 'enc')), may hold values from 1 to 256, as said below
Outputs:
- block_out: bfloat16 [32, 1024, 2432], P(('dp', 'enc'), 'seq')
- d_gate: float32 [32, 2432], P(('dp', 'enc'))
- d_out_weight: float32 [1536, 2432], P(('dp', 'seq', 'enc'))
The draws below stay inside these ranges and needn't reach their ends.
Inputs may be any that keep to these rules, and one draw needn't show every extreme that they name: `caption_len`: some image has all 256 caption slots valid.
All inputs are finite; a program needn't handle non-finite values.
Results may differ from the reference program's by a relative error of at most 0.024.
Values may be sent and summed in bfloat16 or wider, within the bound.
No kernel may reach another device: no remote copies, remote signals or barrier semaphores. Data moves between devices by JAX's collectives and lax.ppermute only.
A program may use at most 128 MiB of HBM per device.

```python
import jax
import jax.numpy as jnp
from jax import lax

D = 2432
HEAD = 64
T5W = 4096
HEADS = 24
HA = 1536
IMAGES = 32
LAT = 1024
TXT = 256


def draw_image_qkv(key, part):
    key = jax.random.fold_in(key, 11)
    shape = (IMAGES, LAT, HEADS, 3, HEAD)
    values = jnp.clip(1.5 * jax.random.normal(key, shape, jnp.float32), -7.0, 7.0)
    return values.reshape(IMAGES, LAT, 3 * HEADS * HEAD).astype(jnp.bfloat16)


def draw_caption_len(key, part):
    key = jax.random.fold_in(key, 5)
    drawn = jax.random.randint(key, (IMAGES,), 1, TXT + 1, dtype=jnp.int32)
    return drawn.at[0].set(TXT)


def shard_levels(stream_key, dims, pieces, low, high):
    gain, own = 1.0, jax.random.fold_in(stream_key, 6)
    for dim, blocks in pieces:
        heights = jnp.exp(jax.random.uniform(jax.random.fold_in(own, dim), (blocks,), jnp.float32, low / len(pieces), high / len(pieces)))
        gain = gain * jnp.repeat(heights, dims[dim] // blocks).reshape([-1 if axis == dim else 1 for axis in range(len(dims))])
    return gain


def noise(key, shape, width, limit, cuts=(), kind=jnp.bfloat16):
    values = width * jax.random.normal(key, shape, jnp.float32)
    if cuts:
        values = values * shard_levels(key, shape, cuts, -0.22, 0.18)
    return jnp.clip(values, -limit, limit).astype(kind)


def setup_inputs(seed: int = 0) -> dict:
    key_list = jax.random.split(jax.random.key(seed), 9)
    image_qkv = draw_image_qkv(jax.random.fold_in(key_list[8], 71), 0)
    residual = noise(key_list[1], (IMAGES, LAT, D), 0.25, 1.5, ((0, 32), (1, 8)))
    gate = jnp.clip(0.5 + 1.5 * jax.random.uniform(key_list[2], (IMAGES, D), jnp.float32) ** shard_levels(key_list[2], (IMAGES, D), ((0, 32),), -0.2, 0.2), 0.5, 2.0)
    cotangent = noise(key_list[3], (IMAGES, LAT, D), 1.0, 6.0, ((0, 32), (1, 8)))
    t5_states = noise(key_list[4], (IMAGES, TXT, T5W), 1.0, 6.0, ((0, 16), (1, 8), (2, 2)))
    text_weight = noise(key_list[5], (2, T5W, HA), T5W ** -0.5, 0.09375, ((1, 2), (2, 8)))
    out_weight = noise(key_list[6], (HA, D), HA ** -0.5, 0.15625, ((0, 256),))
    caption_len = draw_caption_len(jax.random.fold_in(key_list[8], 71), 0)
    return dict(image_qkv=image_qkv, residual=residual, gate=gate, cotangent=cotangent, t5_states=t5_states, text_weight=text_weight, out_weight=out_weight, caption_len=caption_len)


def attend(query, key_img, value_img, key_txt, value_txt, length):
    rows = query.shape[0]
    block = min(512, rows)
    scale = query.shape[2] ** -0.5
    valid = jnp.arange(key_txt.shape[0], dtype=jnp.int32) < length
    kimg = key_img.astype(jnp.float32)
    ktxt = key_txt.astype(jnp.float32)
    vimg = value_img.astype(jnp.float32)
    vtxt = value_txt.astype(jnp.float32)

    def one_block(qblock):
        qf = qblock.astype(jnp.float32)
        s_img = jnp.einsum("qhe,khe->hqk", qf, kimg) * scale
        s_txt = jnp.einsum("qhe,khe->hqk", qf, ktxt) * scale
        s_txt = jnp.where(valid[None, None, :], s_txt, -jnp.inf)
        top = jnp.maximum(jnp.max(s_img, axis=-1, keepdims=True), jnp.max(s_txt, axis=-1, keepdims=True))
        p_img = jnp.exp(s_img - top)
        p_txt = jnp.exp(s_txt - top)
        total = jnp.sum(p_img, axis=-1, keepdims=True) + jnp.sum(p_txt, axis=-1, keepdims=True)
        w_img = (p_img / total).astype(jnp.bfloat16).astype(jnp.float32)
        w_txt = (p_txt / total).astype(jnp.bfloat16).astype(jnp.float32)
        out = jnp.einsum("hqk,khe->qhe", w_img, vimg) + jnp.einsum("hqk,khe->qhe", w_txt, vtxt)
        return out.astype(jnp.bfloat16)

    blocks = query.reshape(rows // block, block, query.shape[1], query.shape[2])
    result = lax.map(one_block, blocks)
    return result.reshape(rows, query.shape[1], query.shape[2])


def reference(image_qkv, residual, gate, cotangent, t5_states, text_weight, out_weight, caption_len):
    text_kv = jnp.einsum("ntf,cfa->ntca", t5_states.astype(jnp.float32), text_weight.astype(jnp.float32)).astype(jnp.bfloat16)
    text_kv = text_kv.reshape(IMAGES, TXT, 2, HEADS, HEAD)
    qkv = image_qkv.reshape(IMAGES, LAT, HEADS, 3, HEAD)

    def per_image(items):
        piece, tkv, length = items
        return attend(piece[:, :, 0], piece[:, :, 1], piece[:, :, 2], tkv[:, 0], tkv[:, 1], length)

    attn = lax.map(per_image, (qkv, text_kv, caption_len))
    attn_flat = attn.reshape(IMAGES * LAT, HA)
    proj = jnp.dot(attn_flat, out_weight, preferred_element_type=jnp.float32).reshape(IMAGES, LAT, D)
    block_out = (residual.astype(jnp.float32) + gate[:, None, :] * proj).astype(jnp.bfloat16)
    d_gate = jnp.sum(cotangent.astype(jnp.float32) * proj, axis=1)
    scaled = (gate[:, None, :] * cotangent.astype(jnp.float32)).astype(jnp.bfloat16)
    d_out_weight = lax.dot_general(attn_flat, scaled.reshape(IMAGES * LAT, D), (((0,), (0,)), ((), ())), preferred_element_type=jnp.float32)
    return block_out, d_gate, d_out_weight
```

```python
import jax
import jax.numpy as jnp
from jax import lax
from jax.sharding import PartitionSpec as P

HEAD = 64
PLANE = ("dp", "enc")
WHOLE = ("dp", "seq", "enc")
DOWN = 4


def attend(query, key, value, bias):
    scale = query.shape[2] ** (-0.5)
    s = jnp.einsum("qhe,khe->hqk", query, key, preferred_element_type=jnp.float32) * scale
    s = s + bias[None, None, :]
    p = jnp.exp(s - jnp.max(s, axis=-1, keepdims=True))
    w = (p / jnp.sum(p, axis=-1, keepdims=True)).astype(jnp.bfloat16)
    out = jnp.einsum("hqk,khe->qhe", w, value, preferred_element_type=jnp.float32)
    return out.astype(jnp.bfloat16)


def per_device(
    image_qkv, residual, gate, cotangent, t5_states, text_weight, out_weight, caption_len
):
    n_dp, n_seq, n_enc = lax.axis_size("dp"), lax.axis_size("seq"), lax.axis_size("enc")
    _, tok, columns = image_qkv.shape
    group = columns // n_seq
    heads = group // (3 * HEAD)
    own_rows, width = out_weight.shape
    enc = lax.axis_index("enc")

    flat = own_rows * width
    lanes = t5_states.shape[2]
    wide = flat // own_rows // lanes * lanes
    narrow = width - wide
    own_txt = t5_states.shape[0] * t5_states.shape[1]

    rest = -(-own_rows * narrow // lanes)
    tail = jnp.pad(out_weight[:, wide:].reshape(-1), (0, rest * lanes - own_rows * narrow))
    packed = jnp.concatenate(
        [t5_states.reshape(own_txt, lanes), out_weight[:, :wide], tail.reshape(rest, lanes)], axis=0
    )
    packed_full = lax.all_gather(packed, "seq", axis=0)
    spread = lax.all_to_all(
        image_qkv.reshape(tok, n_seq, group), "seq", split_axis=1, concat_axis=0, tiled=True
    )
    full = tok * n_seq
    spread = spread.reshape(full, heads, 3, HEAD)

    cot_float = cotangent[0].astype(jnp.float32)
    scaled = (gate * cot_float).astype(jnp.bfloat16)
    blocks = {0: scaled}

    def ring_step(j):
        if j <= DOWN:
            blocks[j] = lax.ppermute(
                blocks[j - 1], "seq", [(i, (i - 1) % n_seq) for i in range(n_seq)]
            )
        if j < n_seq - DOWN:
            blocks[-j] = lax.ppermute(
                blocks[1 - j], "seq", [(i, (i + 1) % n_seq) for i in range(n_seq)]
            )

    def done_with(j, *values):
        mine = [k for k in blocks if abs(k) == j]
        held = lax.optimization_barrier((tuple(blocks[k] for k in mine), values))
        blocks.update(zip(mine, held[0]))
        return held[1]

    ring_step(1)
    packed_full, spread = done_with(1, packed_full, spread)
    ring_step(2)

    t5_full = packed_full[:, :own_txt].reshape(n_seq * own_txt, lanes)
    w_main = packed_full[:, own_txt : own_txt + own_rows]
    w_rest = packed_full[:, own_txt + own_rows :].reshape(n_seq, rest * lanes)
    w_rest = w_rest[:, : own_rows * narrow].reshape(n_seq, own_rows, narrow)
    w_seq = jnp.concatenate([w_main, w_rest], axis=2)
    swap = [(0, 1), (1, 0)]
    w_got = lax.ppermute(w_seq, "enc", swap)
    w_pair = jnp.stack(
        [jnp.where(enc == 0, w_seq, w_got), jnp.where(enc == 0, w_got, w_seq)], axis=1
    )
    w_full = lax.all_gather(
        w_pair.reshape(n_seq * n_enc * own_rows, width), "dp", axis=0, tiled=True
    )
    partial = lax.dot_general(
        t5_full, text_weight, (((1,), (1,)), ((), ())), preferred_element_type=jnp.float32
    )
    partial = partial.reshape(n_seq, 2, -1, 2, heads * HEAD)
    mine = jnp.where(enc == 0, partial[:, 0], partial[:, 1])
    other = jnp.where(enc == 0, partial[:, 1], partial[:, 0]).astype(jnp.bfloat16)
    got = lax.ppermute(other, "enc", swap)
    got, spread = done_with(2, got, spread)
    ring_step(3)
    text_kv = (mine + got.astype(jnp.float32)).astype(jnp.bfloat16)
    txt = text_kv.shape[0] * text_kv.shape[1]
    text_kv = text_kv.reshape(txt, 2, heads, HEAD)

    bias = jnp.concatenate(
        [
            jnp.zeros((full,), jnp.float32),
            jnp.where(jnp.arange(txt, dtype=jnp.int32) < caption_len[0], 0.0, -jnp.inf),
        ]
    )
    key = jnp.concatenate([spread[:, :, 1], text_kv[:, 0]], axis=0)
    value = jnp.concatenate([spread[:, :, 2], text_kv[:, 1]], axis=0)
    attn = attend(spread[:, :, 0], key, value, bias).reshape(full, heads * HEAD)
    (attn,) = done_with(3, attn)
    ring_step(4)
    attn_tok = lax.all_to_all(
        attn.reshape(n_seq, tok, heads * HEAD), "seq", split_axis=0, concat_axis=0
    )
    (attn_tok,) = done_with(4, attn_tok)
    attn_tok = jnp.swapaxes(attn_tok, 0, 1).reshape(tok, n_seq * heads * HEAD)
    proj = jnp.dot(attn_tok, w_full, preferred_element_type=jnp.float32)
    block_out = (residual[0].astype(jnp.float32) + gate * proj).astype(jnp.bfloat16)
    d_gate = jnp.sum(cot_float * proj, axis=0, keepdims=True)
    for bit in (1, 2, 4):
        d_gate = d_gate + lax.ppermute(d_gate, "seq", [(i, i ^ bit) for i in range(n_seq)])

    me = lax.axis_index("seq")
    grad = 0.0
    for j, block in blocks.items():
        rows = lax.dynamic_slice_in_dim(attn, (me + j) % n_seq * tok, tok, axis=0)
        grad = grad + lax.dot_general(
            rows, block, (((0,), (0,)), ((), ())), preferred_element_type=jnp.float32
        )
    grad = grad.astype(jnp.bfloat16)
    pieces = lax.all_to_all(grad.reshape(n_dp * n_enc, own_rows, width), PLANE, 0, 0)
    block = jnp.sum(pieces.astype(jnp.float32), axis=0).astype(jnp.bfloat16)
    perm = [
        ((d * n_seq + s) * n_enc + e, s * n_dp * n_enc + d * n_enc + e)
        for d in range(n_dp)
        for s in range(n_seq)
        for e in range(n_enc)
    ]
    d_out_weight = lax.ppermute(block, WHOLE, perm).astype(jnp.float32)
    return (block_out[None], d_gate, d_out_weight)


def solution(mesh):
    in_specs = (
        P(("dp", "enc"), "seq", None),
        P(("dp", "enc"), "seq", None),
        P(("dp", "enc"), None),
        P(("dp", "enc"), "seq", None),
        P("dp", "seq", "enc"),
        P(None, "enc", "seq"),
        P(("dp", "seq", "enc"), None),
        P(("dp", "enc")),
    )
    out_specs = (
        P(("dp", "enc"), "seq", None),
        P(("dp", "enc"), None),
        P(("dp", "seq", "enc"), None),
    )
    return jax.shard_map(
        per_device, mesh=mesh, in_specs=in_specs, out_specs=out_specs, check_vma=False
    )
```

```python
import functools

import jax
import jax.numpy as jnp
from jax import lax
from jax.experimental import pallas as pl
from jax.experimental.pallas import tpu as pltpu
from jax.sharding import PartitionSpec as P

HEAD = 64
QUERY_ROWS = 256
COLUMNS = 640
PLANE = ("dp", "enc")
WHOLE = ("dp", "seq", "enc")
LOG2E = 1.4426950408889634
DOT_NT = (((1,), (1,)), ((), ()))
DOT_TN = (((0,), (0,)), ((), ()))


def attend_kernel(length_ref, qkv_ref, mine_ref, got_ref, out_ref):
    full, txt = qkv_ref.shape[0], mine_ref.shape[1]
    factor = HEAD ** (-0.5) * LOG2E
    rows = min(QUERY_ROWS, full)
    text_kv = (mine_ref[...] + got_ref[...].astype(jnp.float32)).astype(jnp.bfloat16)
    valid = lax.broadcasted_iota(jnp.int32, (1, txt), 1) < length_ref[0]
    for h in range(out_ref.shape[1] // HEAD):
        base = 3 * h * HEAD
        cols = slice(h * HEAD, (h + 1) * HEAD)
        k_img = qkv_ref[:, base + HEAD : base + 2 * HEAD]
        v_img = qkv_ref[:, base + 2 * HEAD : base + 3 * HEAD]
        k_txt, v_txt = text_kv[0, :, cols], text_kv[1, :, cols]
        for r in range(full // rows):
            q = qkv_ref[r * rows : (r + 1) * rows, base : base + HEAD]
            s_img = lax.dot_general(q, k_img, DOT_NT, preferred_element_type=jnp.float32)
            s_txt = lax.dot_general(q, k_txt, DOT_NT, preferred_element_type=jnp.float32)
            s_txt = jnp.where(valid, s_txt, -jnp.inf)
            top = jnp.maximum(
                jnp.max(s_img, axis=1, keepdims=True), jnp.max(s_txt, axis=1, keepdims=True)
            )
            p_img = jnp.exp2((s_img - top) * factor)
            p_txt = jnp.exp2((s_txt - top) * factor)
            total = jnp.sum(p_img, axis=1, keepdims=True) + jnp.sum(p_txt, axis=1, keepdims=True)
            out = jnp.dot(p_img.astype(jnp.bfloat16), v_img, preferred_element_type=jnp.float32)
            out += jnp.dot(p_txt.astype(jnp.bfloat16), v_txt, preferred_element_type=jnp.float32)
            out_ref[r * rows : (r + 1) * rows, cols] = (out / total).astype(out_ref.dtype)


def attend(length, qkv, mine, got):
    full, group = qkv.shape
    keys = full + mine.shape[1]
    return pl.pallas_call(
        attend_kernel,
        out_shape=jax.ShapeDtypeStruct((full, group // 3), jnp.bfloat16),
        in_specs=[pl.BlockSpec(memory_space=pltpu.SMEM)]
        + [pl.BlockSpec(memory_space=pltpu.VMEM)] * 3,
        out_specs=pl.BlockSpec(memory_space=pltpu.VMEM),
        compiler_params=pltpu.CompilerParams(vmem_limit_bytes=40 * 2**20),
        cost_estimate=pl.CostEstimate(
            flops=4 * full * keys * group // 3,
            bytes_accessed=2 * full * group * 2,
            transcendentals=full * keys * group // (3 * HEAD),
        ),
    )(length, qkv, mine, got)


def grad_kernel(order, start_ref, attn_ref, *refs):
    *block_refs, out_ref = refs
    tok, width = block_refs[0].shape
    count = len(block_refs)
    lhs = []
    for j in order:
        row = lax.rem(start_ref[0] + j + count, count) * tok
        lhs.append(attn_ref[pl.ds(pl.multiple_of(row, tok), tok), :])
    for c in range(0, width, COLUMNS):
        cols = slice(c, min(c + COLUMNS, width))
        total = lax.dot_general(
            lhs[0], block_refs[0][:, cols], DOT_TN, preferred_element_type=jnp.float32
        )
        for rows, ref in zip(lhs[1:], block_refs[1:]):
            total += lax.dot_general(
                rows, ref[:, cols], DOT_TN, preferred_element_type=jnp.float32
            )
        out_ref[:, cols] = total.astype(out_ref.dtype)


def gradient(me, attn, blocks):
    order = sorted(blocks)
    tok, width = blocks[0].shape
    return pl.pallas_call(
        functools.partial(grad_kernel, order),
        out_shape=jax.ShapeDtypeStruct((attn.shape[1], width), jnp.bfloat16),
        in_specs=[pl.BlockSpec(memory_space=pltpu.SMEM)]
        + [pl.BlockSpec(memory_space=pltpu.VMEM)] * (1 + len(order)),
        out_specs=pl.BlockSpec(memory_space=pltpu.VMEM),
        compiler_params=pltpu.CompilerParams(vmem_limit_bytes=40 * 2**20),
        cost_estimate=pl.CostEstimate(
            flops=2 * attn.shape[0] * attn.shape[1] * width,
            bytes_accessed=2 * attn.shape[0] * width,
            transcendentals=0,
        ),
    )(me.reshape(1), attn, *[blocks[j] for j in order])


def per_device(
    image_qkv, residual, gate, cotangent, t5_states, text_weight, out_weight, caption_len
):
    n_dp, n_seq, n_enc = lax.axis_size("dp"), lax.axis_size("seq"), lax.axis_size("enc")
    _, tok, columns = image_qkv.shape
    group = columns // n_seq
    own_rows, width = out_weight.shape
    enc, me = lax.axis_index("enc"), lax.axis_index("seq")
    swap = [(0, 1), (1, 0)]

    w_seq = lax.all_to_all(
        jnp.broadcast_to(out_weight[None], (n_seq, own_rows, width)), "seq", 0, 0
    )
    w_got = lax.ppermute(w_seq, "enc", swap)
    w_pair = jnp.stack(
        [jnp.where(enc == 0, w_seq, w_got), jnp.where(enc == 0, w_got, w_seq)], axis=1
    ).reshape(n_seq * n_enc * own_rows, width)

    t5_full = lax.all_gather(t5_states, "seq", axis=1, tiled=True)
    spread = lax.all_to_all(
        jnp.swapaxes(image_qkv.reshape(tok, n_seq, group), 0, 1), "seq", 0, 0
    )
    spread = spread.reshape(tok * n_seq, group)

    cot_float = cotangent[0].astype(jnp.float32)
    scaled = (gate * cot_float).astype(jnp.bfloat16)
    blocks = {0: scaled}

    def ring_step(j):
        towards = -1 if j > 0 else 1
        blocks[j] = lax.ppermute(
            blocks[j + towards], "seq", [(i, (i + towards) % n_seq) for i in range(n_seq)]
        )

    def done_with(steps, *values):
        held = lax.optimization_barrier((tuple(blocks[j] for j in steps), values))
        blocks.update(zip(steps, held[0]))
        return held[1]

    ring_step(-1)
    ring_step(1)
    t5_full, spread, w_pair = done_with([-1, 1], t5_full, spread, w_pair)
    w_full = lax.all_gather(w_pair, "dp", axis=0, tiled=True)
    ring_step(-2)
    ring_step(2)

    partial = jnp.einsum(
        "ntf,cfa->ncta", t5_full, text_weight, preferred_element_type=jnp.float32
    )
    mine = jnp.where(enc == 0, partial[0], partial[1])
    other = jnp.where(enc == 0, partial[1], partial[0]).astype(jnp.bfloat16)
    got = lax.ppermute(other, "enc", swap)
    (got,) = done_with([-2], got)
    ring_step(-3)

    attn = attend(caption_len, spread, mine, got)
    (attn,) = done_with([-3, 2], attn)
    ring_step(-4)
    ring_step(3)

    attn_tok = lax.all_to_all(
        attn.reshape(n_seq, tok, group // 3), "seq", split_axis=0, concat_axis=0
    )
    attn_tok = jnp.swapaxes(attn_tok, 0, 1).reshape(tok, columns // 3)

    grad = gradient(me, attn, blocks)
    pieces = lax.all_to_all(grad.reshape(n_dp * n_enc, own_rows, width), PLANE, 0, 0)
    proj = jnp.dot(attn_tok, w_full, preferred_element_type=jnp.float32)
    block_out = (residual[0].astype(jnp.float32) + gate * proj).astype(jnp.bfloat16)
    d_gate = jnp.sum(cot_float * proj, axis=0, keepdims=True)
    bit = 1
    while bit < n_seq:
        d_gate = d_gate + lax.ppermute(d_gate, "seq", [(i, i ^ bit) for i in range(n_seq)])
        bit *= 2
    pieces, d_gate = lax.optimization_barrier((pieces, d_gate))
    block = jnp.sum(pieces.astype(jnp.float32), axis=0).astype(jnp.bfloat16)
    perm = [
        ((d * n_seq + s) * n_enc + e, s * n_dp * n_enc + d * n_enc + e)
        for d in range(n_dp)
        for s in range(n_seq)
        for e in range(n_enc)
    ]
    d_out_weight = lax.ppermute(block, WHOLE, perm).astype(jnp.float32)
    return (block_out[None], d_gate, d_out_weight)


def solution(mesh):
    in_specs = (
        P(("dp", "enc"), "seq", None),
        P(("dp", "enc"), "seq", None),
        P(("dp", "enc"), None),
        P(("dp", "enc"), "seq", None),
        P("dp", "seq", "enc"),
        P(None, "enc", "seq"),
        P(("dp", "seq", "enc"), None),
        P(("dp", "enc")),
    )
    out_specs = (
        P(("dp", "enc"), "seq", None),
        P(("dp", "enc"), None),
        P(("dp", "seq", "enc"), None),
    )
    return jax.shard_map(
        per_device, mesh=mesh, in_specs=in_specs, out_specs=out_specs, check_vma=False
    )
```

```python
import functools

import jax
import jax.numpy as jnp
from jax import lax
from jax.experimental import pallas as pl
from jax.experimental.pallas import tpu as pltpu
from jax.sharding import PartitionSpec as P

HEAD = 64
QUERY_ROWS = 256
COLUMNS = 640
PLANE = ("dp", "enc")
WHOLE = ("dp", "seq", "enc")
LOG2E = 1.4426950408889634
DOT_NT = (((1,), (1,)), ((), ()))
DOT_TN = (((0,), (0,)), ((), ()))


def attend_kernel(length_ref, qkv_ref, mine_ref, got_ref, out_ref):
    full, txt = qkv_ref.shape[0], mine_ref.shape[1]
    factor = HEAD ** (-0.5) * LOG2E
    rows = min(QUERY_ROWS, full)
    text_kv = (mine_ref[...] + got_ref[...].astype(jnp.float32)).astype(jnp.bfloat16)
    valid = lax.broadcasted_iota(jnp.int32, (1, txt), 1) < length_ref[0]
    for h in range(out_ref.shape[1] // HEAD):
        base = 3 * h * HEAD
        cols = slice(h * HEAD, (h + 1) * HEAD)
        k_img = qkv_ref[:, base + HEAD : base + 2 * HEAD]
        v_img = qkv_ref[:, base + 2 * HEAD : base + 3 * HEAD]
        k_txt, v_txt = text_kv[0, :, cols], text_kv[1, :, cols]
        for r in range(full // rows):
            q = qkv_ref[r * rows : (r + 1) * rows, base : base + HEAD]
            s_img = lax.dot_general(q, k_img, DOT_NT, preferred_element_type=jnp.float32)
            s_txt = lax.dot_general(q, k_txt, DOT_NT, preferred_element_type=jnp.float32)
            s_txt = jnp.where(valid, s_txt, -jnp.inf)
            top = jnp.maximum(
                jnp.max(s_img, axis=1, keepdims=True), jnp.max(s_txt, axis=1, keepdims=True)
            )
            p_img = jnp.exp2((s_img - top) * factor)
            p_txt = jnp.exp2((s_txt - top) * factor)
            total = jnp.sum(p_img, axis=1, keepdims=True) + jnp.sum(p_txt, axis=1, keepdims=True)
            out = jnp.dot(p_img.astype(jnp.bfloat16), v_img, preferred_element_type=jnp.float32)
            out += jnp.dot(p_txt.astype(jnp.bfloat16), v_txt, preferred_element_type=jnp.float32)
            out_ref[r * rows : (r + 1) * rows, cols] = (out / total).astype(out_ref.dtype)


def attend(length, qkv, mine, got):
    full, group = qkv.shape
    keys = full + mine.shape[1]
    return pl.pallas_call(
        attend_kernel,
        out_shape=jax.ShapeDtypeStruct((full, group // 3), jnp.bfloat16),
        in_specs=[pl.BlockSpec(memory_space=pltpu.SMEM)]
        + [pl.BlockSpec(memory_space=pltpu.VMEM)] * 3,
        out_specs=pl.BlockSpec(memory_space=pltpu.VMEM),
        compiler_params=pltpu.CompilerParams(vmem_limit_bytes=40 * 2**20),
        cost_estimate=pl.CostEstimate(
            flops=4 * full * keys * group // 3,
            bytes_accessed=2 * full * group * 2,
            transcendentals=full * keys * group // (3 * HEAD),
        ),
    )(length, qkv, mine, got)


def grad_kernel(places, count, start_ref, attn_ref, *refs):
    block_refs, before_refs, out_ref = refs[: len(places)], refs[len(places) : -1], refs[-1]
    tok, width = attn_ref.shape[0] // count, out_ref.shape[1]
    lhs = []
    for (j, first), ref in zip(places, block_refs):
        rows = ref.shape[0]
        row = lax.rem(start_ref[0] + j + count, count) * tok + first
        lhs.append(attn_ref[pl.ds(pl.multiple_of(row, rows), rows), :])
    for c in range(0, width, COLUMNS):
        cols = slice(c, min(c + COLUMNS, width))
        parts = [
            lax.dot_general(rows, ref[:, cols], DOT_TN, preferred_element_type=jnp.float32)
            for rows, ref in zip(lhs, block_refs)
        ]
        out_ref[:, cols] = sum(parts[1:] + [r[:, cols] for r in before_refs], parts[0]).astype(
            out_ref.dtype
        )


def gradient(me, count, attn, blocks, dtype, *before):
    places, arrays = list(blocks), list(blocks.values())
    width = arrays[0].shape[1]
    rows = sum(a.shape[0] for a in arrays)
    return pl.pallas_call(
        functools.partial(grad_kernel, places, count),
        out_shape=jax.ShapeDtypeStruct((attn.shape[1], width), dtype),
        in_specs=[pl.BlockSpec(memory_space=pltpu.SMEM)]
        + [pl.BlockSpec(memory_space=pltpu.VMEM)] * (1 + len(arrays) + len(before)),
        out_specs=pl.BlockSpec(memory_space=pltpu.VMEM),
        compiler_params=pltpu.CompilerParams(vmem_limit_bytes=40 * 2**20),
        cost_estimate=pl.CostEstimate(
            flops=2 * rows * attn.shape[1] * width,
            bytes_accessed=2 * rows * width,
            transcendentals=0,
        ),
    )(me.reshape(1), attn, *arrays, *before)


def per_device(
    image_qkv, residual, gate, cotangent, t5_states, text_weight, out_weight, caption_len
):
    n_dp, n_seq, n_enc = lax.axis_size("dp"), lax.axis_size("seq"), lax.axis_size("enc")
    _, tok, columns = image_qkv.shape
    group = columns // n_seq
    own_rows, width = out_weight.shape
    enc, me = lax.axis_index("enc"), lax.axis_index("seq")
    swap = [(0, 1), (1, 0)]

    w_seq = lax.all_to_all(
        jnp.broadcast_to(out_weight[None], (n_seq, own_rows, width)), "seq", 0, 0
    )
    w_got = lax.ppermute(w_seq, "enc", swap)
    w_pair = jnp.stack(
        [jnp.where(enc == 0, w_seq, w_got), jnp.where(enc == 0, w_got, w_seq)], axis=1
    ).reshape(n_seq * n_enc * own_rows, width)

    cot_float = cotangent[0].astype(jnp.float32)
    scaled = (gate * cot_float).astype(jnp.bfloat16)
    blocks = {0: scaled}

    def send(block, towards):
        return lax.ppermute(block, "seq", [(i, (i + towards) % n_seq) for i in range(n_seq)])

    def ring_step(j):
        towards = -1 if j > 0 else 1
        blocks[j] = send(blocks[j + towards], towards)

    def done_with(steps, *values):
        held = lax.optimization_barrier((tuple(blocks[j] for j in steps), values))
        blocks.update(zip(steps, held[0]))
        return held[1]

    ring_step(-1)
    ring_step(1)

    t5_full = lax.all_gather(t5_states, "seq", axis=1, tiled=True)
    (image_qkv,) = done_with([-1, 1], image_qkv)
    spread = lax.all_to_all(
        jnp.swapaxes(image_qkv.reshape(tok, n_seq, group), 0, 1), "seq", 0, 0
    )
    spread = spread.reshape(tok * n_seq, group)

    ring_step(-2)
    ring_step(2)
    t5_full, spread, w_pair = lax.optimization_barrier((t5_full, spread, w_pair))
    w_full = lax.all_gather(w_pair, "dp", axis=0, tiled=True)

    partial = jnp.einsum(
        "ntf,cfa->ncta", t5_full, text_weight, preferred_element_type=jnp.float32
    )
    mine = jnp.where(enc == 0, partial[0], partial[1])
    other = jnp.where(enc == 0, partial[1], partial[0]).astype(jnp.bfloat16)
    got = lax.ppermute(other, "enc", swap)
    (got,) = done_with([-2, 2], got)
    ring_step(-3)
    ring_step(3)

    attn = attend(caption_len, spread, mine, got)
    (attn,) = done_with([-3, 3], attn)
    last = n_seq // 2
    opposite = {
        (last, 0): send(blocks[1 - last][: tok // 2], 1),
        (last, tok // 2): send(blocks[last - 1][tok // 2 :], -1),
    }

    attn_tok = lax.all_to_all(
        attn.reshape(n_seq, tok, group // 3), "seq", split_axis=0, concat_axis=0
    )
    attn_tok = jnp.swapaxes(attn_tok, 0, 1).reshape(tok, columns // 3)

    grad = gradient(me, n_seq, attn, {(j, 0): b for j, b in blocks.items()}, jnp.float32)
    grad = gradient(me, n_seq, attn, opposite, jnp.bfloat16, grad)
    pieces = lax.all_to_all(grad.reshape(n_dp * n_enc, own_rows, width), PLANE, 0, 0)
    proj = jnp.dot(attn_tok, w_full, preferred_element_type=jnp.float32)
    block_out = (residual[0].astype(jnp.float32) + gate * proj).astype(jnp.bfloat16)
    d_gate = jnp.sum(cot_float * proj, axis=0, keepdims=True)
    bit = 1
    while bit < n_seq:
        d_gate = d_gate + lax.ppermute(d_gate, "seq", [(i, i ^ bit) for i in range(n_seq)])
        bit *= 2
    pieces, d_gate = lax.optimization_barrier((pieces, d_gate))
    block = jnp.sum(pieces.astype(jnp.float32), axis=0).astype(jnp.bfloat16)
    perm = [
        ((d * n_seq + s) * n_enc + e, s * n_dp * n_enc + d * n_enc + e)
        for d in range(n_dp)
        for s in range(n_seq)
        for e in range(n_enc)
    ]
    d_out_weight = lax.ppermute(block, WHOLE, perm).astype(jnp.float32)
    return (block_out[None], d_gate, d_out_weight)


def solution(mesh):
    in_specs = (
        P(("dp", "enc"), "seq", None),
        P(("dp", "enc"), "seq", None),
        P(("dp", "enc"), None),
        P(("dp", "enc"), "seq", None),
        P("dp", "seq", "enc"),
        P(None, "enc", "seq"),
        P(("dp", "seq", "enc"), None),
        P(("dp", "enc")),
    )
    out_specs = (
        P(("dp", "enc"), "seq", None),
        P(("dp", "enc"), None),
        P(("dp", "seq", "enc"), None),
    )
    return jax.shard_map(
        per_device, mesh=mesh, in_specs=in_specs, out_specs=out_specs, check_vma=False
    )
```

```python
import functools

import jax
import jax.numpy as jnp
from jax import lax
from jax.experimental import pallas as pl
from jax.experimental.pallas import tpu as pltpu
from jax.sharding import PartitionSpec as P

HEAD = 64
QUERY_ROWS = 256
COLUMNS = 640
PLANE = ("dp", "enc")
WHOLE = ("dp", "seq", "enc")
LOG2E = 1.4426950408889634
DOT_NT = (((1,), (1,)), ((), ()))
DOT_TN = (((0,), (0,)), ((), ()))


def attend_kernel(length_ref, qkv_ref, mine_ref, got_ref, out_ref):
    full, txt = qkv_ref.shape[0], mine_ref.shape[1]
    factor = HEAD ** (-0.5) * LOG2E
    rows = min(QUERY_ROWS, full)
    text_kv = (mine_ref[...] + got_ref[...].astype(jnp.float32)).astype(jnp.bfloat16)
    valid = lax.broadcasted_iota(jnp.int32, (1, txt), 1) < length_ref[0]
    for h in range(out_ref.shape[1] // HEAD):
        base = 3 * h * HEAD
        cols = slice(h * HEAD, (h + 1) * HEAD)
        k_img = qkv_ref[:, base + HEAD : base + 2 * HEAD]
        v_img = qkv_ref[:, base + 2 * HEAD : base + 3 * HEAD]
        k_txt, v_txt = text_kv[0, :, cols], text_kv[1, :, cols]
        for r in range(full // rows):
            q = qkv_ref[r * rows : (r + 1) * rows, base : base + HEAD]
            s_img = lax.dot_general(q, k_img, DOT_NT, preferred_element_type=jnp.float32)
            s_txt = lax.dot_general(q, k_txt, DOT_NT, preferred_element_type=jnp.float32)
            s_txt = jnp.where(valid, s_txt, -jnp.inf)
            top = jnp.maximum(
                jnp.max(s_img, axis=1, keepdims=True), jnp.max(s_txt, axis=1, keepdims=True)
            )
            p_img = jnp.exp2((s_img - top) * factor)
            p_txt = jnp.exp2((s_txt - top) * factor)
            total = jnp.sum(p_img, axis=1, keepdims=True) + jnp.sum(p_txt, axis=1, keepdims=True)
            out = jnp.dot(p_img.astype(jnp.bfloat16), v_img, preferred_element_type=jnp.float32)
            out += jnp.dot(p_txt.astype(jnp.bfloat16), v_txt, preferred_element_type=jnp.float32)
            out_ref[r * rows : (r + 1) * rows, cols] = (out / total).astype(out_ref.dtype)


def attend(length, qkv, mine, got):
    full, group = qkv.shape
    keys = full + mine.shape[1]
    return pl.pallas_call(
        attend_kernel,
        out_shape=jax.ShapeDtypeStruct((full, group // 3), jnp.bfloat16),
        in_specs=[pl.BlockSpec(memory_space=pltpu.SMEM)]
        + [pl.BlockSpec(memory_space=pltpu.VMEM)] * 3,
        out_specs=pl.BlockSpec(memory_space=pltpu.VMEM),
        compiler_params=pltpu.CompilerParams(vmem_limit_bytes=40 * 2**20),
        cost_estimate=pl.CostEstimate(
            flops=4 * full * keys * group // 3,
            bytes_accessed=2 * full * group * 2,
            transcendentals=full * keys * group // (3 * HEAD),
        ),
    )(length, qkv, mine, got)


def grad_kernel(places, count, start_ref, attn_ref, *refs):
    block_refs, before_refs, out_ref = refs[: len(places)], refs[len(places) : -1], refs[-1]
    tok, width = attn_ref.shape[0] // count, out_ref.shape[1]
    lhs = []
    for (j, first), ref in zip(places, block_refs):
        rows = ref.shape[0]
        row = lax.rem(start_ref[0] + j + count, count) * tok + first
        lhs.append(attn_ref[pl.ds(pl.multiple_of(row, rows), rows), :])
    for c in range(0, width, COLUMNS):
        cols = slice(c, min(c + COLUMNS, width))
        parts = [
            lax.dot_general(rows, ref[:, cols], DOT_TN, preferred_element_type=jnp.float32)
            for rows, ref in zip(lhs, block_refs)
        ]
        out_ref[:, cols] = sum(parts[1:] + [r[:, cols] for r in before_refs], parts[0]).astype(
            out_ref.dtype
        )


def gradient(me, count, attn, blocks, dtype, *before):
    places, arrays = list(blocks), list(blocks.values())
    width = arrays[0].shape[1]
    rows = sum(a.shape[0] for a in arrays)
    return pl.pallas_call(
        functools.partial(grad_kernel, places, count),
        out_shape=jax.ShapeDtypeStruct((attn.shape[1], width), dtype),
        in_specs=[pl.BlockSpec(memory_space=pltpu.SMEM)]
        + [pl.BlockSpec(memory_space=pltpu.VMEM)] * (1 + len(arrays) + len(before)),
        out_specs=pl.BlockSpec(memory_space=pltpu.VMEM),
        compiler_params=pltpu.CompilerParams(vmem_limit_bytes=40 * 2**20),
        cost_estimate=pl.CostEstimate(
            flops=2 * rows * attn.shape[1] * width,
            bytes_accessed=2 * rows * width,
            transcendentals=0,
        ),
    )(me.reshape(1), attn, *arrays, *before)


def per_device(
    image_qkv, residual, gate, cotangent, t5_states, text_weight, out_weight, caption_len
):
    n_dp, n_seq, n_enc = lax.axis_size("dp"), lax.axis_size("seq"), lax.axis_size("enc")
    _, tok, columns = image_qkv.shape
    group = columns // n_seq
    own_rows, width = out_weight.shape
    enc, me = lax.axis_index("enc"), lax.axis_index("seq")
    swap = [(0, 1), (1, 0)]

    w_seq = lax.all_to_all(
        jnp.broadcast_to(out_weight[None], (n_seq, own_rows, width)), "seq", 0, 0
    )
    w_got = lax.ppermute(w_seq, "enc", swap)
    w_pair = jnp.stack(
        [jnp.where(enc == 0, w_seq, w_got), jnp.where(enc == 0, w_got, w_seq)], axis=1
    ).reshape(n_seq * n_enc * own_rows, width)

    cot_float = cotangent[0].astype(jnp.float32)
    scaled = (gate * cot_float).astype(jnp.bfloat16)
    blocks = {0: scaled}

    def send(block, towards):
        return lax.ppermute(block, "seq", [(i, (i + towards) % n_seq) for i in range(n_seq)])

    def ring_step(j):
        towards = -1 if j > 0 else 1
        blocks[j] = send(blocks[j + towards], towards)

    def done_with(steps, *values):
        held = lax.optimization_barrier((tuple(blocks[j] for j in steps), values))
        blocks.update(zip(steps, held[0]))
        return held[1]

    ring_step(-1)
    ring_step(1)

    t5_full = lax.all_gather(t5_states, "seq", axis=1, tiled=True)
    (image_qkv,) = done_with([-1, 1], image_qkv)
    spread = lax.all_to_all(
        jnp.swapaxes(image_qkv.reshape(tok, n_seq, group), 0, 1), "seq", 0, 0
    )
    spread = spread.reshape(tok * n_seq, group)

    ring_step(-2)
    ring_step(2)
    t5_full, spread, w_pair = lax.optimization_barrier((t5_full, spread, w_pair))
    w_full = lax.all_gather(w_pair, "dp", axis=0, tiled=True)

    partial = jnp.einsum(
        "ntf,cfa->ncta", t5_full, text_weight, preferred_element_type=jnp.float32
    )
    mine = jnp.where(enc == 0, partial[0], partial[1])
    other = jnp.where(enc == 0, partial[1], partial[0]).astype(jnp.bfloat16)
    got = lax.ppermute(other, "enc", swap)
    (got,) = done_with([-2, 2], got)
    ring_step(-3)
    ring_step(3)

    attn = attend(caption_len, spread, mine, got)
    (attn,) = done_with([-3, 3], attn)
    last = n_seq // 2
    opposite = {
        (last, 0): send(blocks[1 - last][: tok // 2], 1),
        (last, tok // 2): send(blocks[last - 1][tok // 2 :], -1),
    }

    attn_tok = lax.all_to_all(
        attn.reshape(n_seq, tok, group // 3), "seq", split_axis=0, concat_axis=0
    )
    attn_tok = jnp.swapaxes(attn_tok, 0, 1).reshape(tok, columns // 3)

    grad = gradient(me, n_seq, attn, {(j, 0): b for j, b in blocks.items()}, jnp.float32)
    grad = gradient(me, n_seq, attn, opposite, jnp.bfloat16, grad)
    pieces = lax.all_to_all(grad.reshape(n_dp * n_enc, own_rows, width), PLANE, 0, 0)
    proj = jnp.dot(attn_tok, w_full, preferred_element_type=jnp.float32)
    block_out = (residual[0].astype(jnp.float32) + gate * proj).astype(jnp.bfloat16)
    d_gate = jnp.sum(cot_float * proj, axis=0, keepdims=True)
    bit = 1
    while bit < n_seq:
        if 2 * bit == n_seq:
            pieces, d_gate = lax.optimization_barrier((pieces, d_gate))
        d_gate = d_gate + lax.ppermute(d_gate, "seq", [(i, i ^ bit) for i in range(n_seq)])
        bit *= 2
    block = jnp.sum(pieces.astype(jnp.float32), axis=0).astype(jnp.bfloat16)
    perm = [
        ((d * n_seq + s) * n_enc + e, s * n_dp * n_enc + d * n_enc + e)
        for d in range(n_dp)
        for s in range(n_seq)
        for e in range(n_enc)
    ]
    d_out_weight = lax.ppermute(block, WHOLE, perm).astype(jnp.float32)
    return (block_out[None], d_gate, d_out_weight)


def solution(mesh):
    in_specs = (
        P(("dp", "enc"), "seq", None),
        P(("dp", "enc"), "seq", None),
        P(("dp", "enc"), None),
        P(("dp", "enc"), "seq", None),
        P("dp", "seq", "enc"),
        P(None, "enc", "seq"),
        P(("dp", "seq", "enc"), None),
        P(("dp", "enc")),
    )
    out_specs = (
        P(("dp", "enc"), "seq", None),
        P(("dp", "enc"), None),
        P(("dp", "seq", "enc"), None),
    )
    return jax.shard_map(
        per_device, mesh=mesh, in_specs=in_specs, out_specs=out_specs, check_vma=False
    )
```

```python
import functools

import jax
import jax.numpy as jnp
from jax import lax
from jax.experimental import pallas as pl
from jax.experimental.pallas import tpu as pltpu
from jax.sharding import PartitionSpec as P

HEAD = 64
QUERY_ROWS = 256
COLUMNS = 640
PLANE = ("dp", "enc")
WHOLE = ("dp", "seq", "enc")
LOG2E = 1.4426950408889634
DOT_NT = (((1,), (1,)), ((), ()))
DOT_TN = (((0,), (0,)), ((), ()))


def attend_kernel(length_ref, qkv_ref, mine_ref, got_ref, out_ref):
    full, txt = qkv_ref.shape[0], mine_ref.shape[1]
    factor = HEAD ** (-0.5) * LOG2E
    rows = min(QUERY_ROWS, full)
    text_kv = (mine_ref[...] + got_ref[...].astype(jnp.float32)).astype(jnp.bfloat16)
    valid = lax.broadcasted_iota(jnp.int32, (1, txt), 1) < length_ref[0]
    for h in range(out_ref.shape[1] // HEAD):
        base = 3 * h * HEAD
        cols = slice(h * HEAD, (h + 1) * HEAD)
        k_img = qkv_ref[:, base + HEAD : base + 2 * HEAD]
        v_img = qkv_ref[:, base + 2 * HEAD : base + 3 * HEAD]
        k_txt, v_txt = text_kv[0, :, cols], text_kv[1, :, cols]
        for r in range(full // rows):
            q = qkv_ref[r * rows : (r + 1) * rows, base : base + HEAD]
            s_img = lax.dot_general(q, k_img, DOT_NT, preferred_element_type=jnp.float32)
            s_txt = lax.dot_general(q, k_txt, DOT_NT, preferred_element_type=jnp.float32)
            s_txt = jnp.where(valid, s_txt, -jnp.inf)
            top = jnp.maximum(
                jnp.max(s_img, axis=1, keepdims=True), jnp.max(s_txt, axis=1, keepdims=True)
            )
            p_img = jnp.exp2((s_img - top) * factor)
            p_txt = jnp.exp2((s_txt - top) * factor)
            total = jnp.sum(p_img, axis=1, keepdims=True) + jnp.sum(p_txt, axis=1, keepdims=True)
            out = jnp.dot(p_img.astype(jnp.bfloat16), v_img, preferred_element_type=jnp.float32)
            out += jnp.dot(p_txt.astype(jnp.bfloat16), v_txt, preferred_element_type=jnp.float32)
            out_ref[r * rows : (r + 1) * rows, cols] = (out / total).astype(out_ref.dtype)


def attend(length, qkv, mine, got):
    full, group = qkv.shape
    keys = full + mine.shape[1]
    return pl.pallas_call(
        attend_kernel,
        out_shape=jax.ShapeDtypeStruct((full, group // 3), jnp.bfloat16),
        in_specs=[pl.BlockSpec(memory_space=pltpu.SMEM)]
        + [pl.BlockSpec(memory_space=pltpu.VMEM)] * 3,
        out_specs=pl.BlockSpec(memory_space=pltpu.VMEM),
        compiler_params=pltpu.CompilerParams(vmem_limit_bytes=40 * 2**20),
        cost_estimate=pl.CostEstimate(
            flops=4 * full * keys * group // 3,
            bytes_accessed=2 * full * group * 2,
            transcendentals=full * keys * group // (3 * HEAD),
        ),
    )(length, qkv, mine, got)


def grad_kernel(places, count, start_ref, attn_ref, *refs):
    block_refs, before_refs, out_ref = refs[: len(places)], refs[len(places) : -1], refs[-1]
    tok, width = attn_ref.shape[0] // count, out_ref.shape[1]
    lhs = []
    for (j, first), ref in zip(places, block_refs):
        rows = ref.shape[0]
        row = lax.rem(start_ref[0] + j + count, count) * tok + first
        lhs.append(attn_ref[pl.ds(pl.multiple_of(row, rows), rows), :])
    for c in range(0, width, COLUMNS):
        cols = slice(c, min(c + COLUMNS, width))
        parts = [
            lax.dot_general(rows, ref[:, cols], DOT_TN, preferred_element_type=jnp.float32)
            for rows, ref in zip(lhs, block_refs)
        ]
        out_ref[:, cols] = sum(parts[1:] + [r[:, cols] for r in before_refs], parts[0]).astype(
            out_ref.dtype
        )


def gradient(me, count, attn, blocks, dtype, *before):
    places, arrays = list(blocks), list(blocks.values())
    width = arrays[0].shape[1]
    rows = sum(a.shape[0] for a in arrays)
    return pl.pallas_call(
        functools.partial(grad_kernel, places, count),
        out_shape=jax.ShapeDtypeStruct((attn.shape[1], width), dtype),
        in_specs=[pl.BlockSpec(memory_space=pltpu.SMEM)]
        + [pl.BlockSpec(memory_space=pltpu.VMEM)] * (1 + len(arrays) + len(before)),
        out_specs=pl.BlockSpec(memory_space=pltpu.VMEM),
        compiler_params=pltpu.CompilerParams(vmem_limit_bytes=(40 if before else 58) * 2**20),
        cost_estimate=pl.CostEstimate(
            flops=2 * rows * attn.shape[1] * width,
            bytes_accessed=2 * rows * width,
            transcendentals=0,
        ),
    )(me.reshape(1), attn, *arrays, *before)


def per_device(
    image_qkv, residual, gate, cotangent, t5_states, text_weight, out_weight, caption_len
):
    n_dp, n_seq, n_enc = lax.axis_size("dp"), lax.axis_size("seq"), lax.axis_size("enc")
    _, tok, columns = image_qkv.shape
    group = columns // n_seq
    own_rows, width = out_weight.shape
    enc, me = lax.axis_index("enc"), lax.axis_index("seq")
    swap = [(0, 1), (1, 0)]

    w_seq = lax.all_to_all(
        jnp.broadcast_to(out_weight[None], (n_seq, own_rows, width)), "seq", 0, 0
    )
    w_got = lax.ppermute(w_seq, "enc", swap)
    w_pair = jnp.stack(
        [jnp.where(enc == 0, w_seq, w_got), jnp.where(enc == 0, w_got, w_seq)], axis=1
    ).reshape(n_seq * n_enc * own_rows, width)

    cot_float = cotangent[0].astype(jnp.float32)
    scaled = (gate * cot_float).astype(jnp.bfloat16)
    blocks = {0: scaled}

    def send(block, towards):
        return lax.ppermute(block, "seq", [(i, (i + towards) % n_seq) for i in range(n_seq)])

    def ring_step(j):
        towards = -1 if j > 0 else 1
        blocks[j] = send(blocks[j + towards], towards)

    def done_with(steps, *values):
        held = lax.optimization_barrier((tuple(blocks[j] for j in steps), values))
        blocks.update(zip(steps, held[0]))
        return held[1]

    ring_step(-1)
    ring_step(1)

    t5_full = lax.all_gather(t5_states, "seq", axis=1, tiled=True)
    (image_qkv,) = done_with([-1, 1], image_qkv)
    spread = lax.all_to_all(
        jnp.swapaxes(image_qkv.reshape(tok, n_seq, group), 0, 1), "seq", 0, 0
    )
    spread = spread.reshape(tok * n_seq, group)

    ring_step(-2)
    ring_step(2)
    t5_full, spread, w_pair = lax.optimization_barrier((t5_full, spread, w_pair))
    w_full = lax.all_gather(w_pair, "dp", axis=0, tiled=True)

    partial = jnp.einsum(
        "ntf,cfa->ncta", t5_full, text_weight, preferred_element_type=jnp.float32
    )
    mine = jnp.where(enc == 0, partial[0], partial[1])
    other = jnp.where(enc == 0, partial[1], partial[0]).astype(jnp.bfloat16)
    got = lax.ppermute(other, "enc", swap)
    (got,) = done_with([-2, 2], got)
    ring_step(-3)
    ring_step(3)

    attn = attend(caption_len, spread, mine, got)
    (attn,) = done_with([-3, 3], attn)
    last = n_seq // 2
    opposite = {
        (last, 0): send(blocks[1 - last][: tok // 2], 1),
        (last, tok // 2): send(blocks[last - 1][tok // 2 :], -1),
    }

    attn_tok = lax.all_to_all(
        attn.reshape(n_seq, tok, group // 3), "seq", split_axis=0, concat_axis=0
    )
    attn_tok = jnp.swapaxes(attn_tok, 0, 1).reshape(tok, columns // 3)

    grad = gradient(me, n_seq, attn, {(j, 0): b for j, b in blocks.items()}, jnp.float32)
    grad = gradient(me, n_seq, attn, opposite, jnp.bfloat16, grad)
    pieces = lax.all_to_all(grad.reshape(n_dp * n_enc, own_rows, width), PLANE, 0, 0)
    proj = jnp.dot(attn_tok, w_full, preferred_element_type=jnp.float32)
    block_out = (residual[0].astype(jnp.float32) + gate * proj).astype(jnp.bfloat16)
    d_gate = jnp.sum(cot_float * proj, axis=0, keepdims=True)
    bit = 1
    while bit < n_seq:
        if 2 * bit == n_seq:
            pieces, d_gate = lax.optimization_barrier((pieces, d_gate))
        d_gate = d_gate + lax.ppermute(d_gate, "seq", [(i, i ^ bit) for i in range(n_seq)])
        bit *= 2
    block = jnp.sum(pieces.astype(jnp.float32), axis=0).astype(jnp.bfloat16)
    perm = [
        ((d * n_seq + s) * n_enc + e, s * n_dp * n_enc + d * n_enc + e)
        for d in range(n_dp)
        for s in range(n_seq)
        for e in range(n_enc)
    ]
    d_out_weight = lax.ppermute(block, WHOLE, perm).astype(jnp.float32)
    return (block_out[None], d_gate, d_out_weight)


def solution(mesh):
    in_specs = (
        P(("dp", "enc"), "seq", None),
        P(("dp", "enc"), "seq", None),
        P(("dp", "enc"), None),
        P(("dp", "enc"), "seq", None),
        P("dp", "seq", "enc"),
        P(None, "enc", "seq"),
        P(("dp", "seq", "enc"), None),
        P(("dp", "enc")),
    )
    out_specs = (
        P(("dp", "enc"), "seq", None),
        P(("dp", "enc"), None),
        P(("dp", "seq", "enc"), None),
    )
    return jax.shard_map(
        per_device, mesh=mesh, in_specs=in_specs, out_specs=out_specs, check_vma=False
    )
```
